32 devices in a mesh: rep: 2 (over y), tract: 4 (over x, core), head: 4 (over z).
Axes of the slice: x: 2, y: 2, z: 4, core: 2. Of those that a mesh axis runs over, the one named last changes fastest.
Arguments:
- frames: bfloat16 [8, 256, 6144], P(('rep', 'tract'), 'head'), parts along dimension 0, may hold values from -7 to 7
- levels: int32 [8], P(('rep', 'tract')), parts along dimension 0, may hold values from 0 to 7
- visible: int32 [8, 4], P(('rep', 'tract')), parts along dimension 0, may hold values from 0 to 1, as said below
- w_qkv: bfloat16 [6144, 3, 1024], P(None, None, 'head'), may hold values from -0.2 to 0.2
- w_out: bfloat16 [1024, 6144], P('head'), may hold values from -1.5 to 1.5
- modulation: float32 [8, 3, 6144], replicated, may hold values from -3 to 3
Outputs:
- mixed: bfloat16 [8, 256, 6144], P(('rep', 'tract'), 'head'), parts along dimension 0
The draws below stay inside these ranges and needn't reach their ends.
There are 2 independent parts, one for each index of `rep`. The reference program is written for one: setup_inputs(seed, part) draws one part's arguments, and reference() takes and returns one part's arrays. A program takes and returns all parts, laid end to end along the dimension named above; an argument that names none is the same for every part. Nothing has to cross between parts.
Inputs may be any that keep to these rules, and one draw needn't show every extreme that they name: visible[c, c] is 1 and visible[c, j] is 0 for every j > c.
All inputs are finite; a program needn't handle non-finite values.
Results may differ from the reference program's by a relative error of at most 0.019.
Values may be sent and summed in bfloat16 or wider, within the bound.
No kernel may reach another device: no remote copies, remote signals or barrier semaphores. Data moves between devices by JAX's collectives and lax.ppermute only.
A program may use at most 64 MiB of HBM per device.

```python
import jax
import jax.numpy as jnp
from jax import lax

D = 6144
HD = 128
H_DEV = 2
CT = 256
NSTEP = 8
HEADS = 8
NCHUNK = 4
N_HEAD = 4


def draw_frames(key, part):
    base = jax.random.normal(jax.random.fold_in(key, 11), (NCHUNK, CT, D), jnp.float32)
    return jnp.clip(base, -6.5, 6.5).astype(jnp.bfloat16)


def draw_w_qkv(key, part):
    spread = D ** (-0.5)
    queries = spread * jax.random.normal(jax.random.fold_in(key, 21), (D, HEADS * HD), jnp.float32)
    key_part = spread * jax.random.normal(jax.random.fold_in(key, 22), (D, HEADS * HD), jnp.float32)
    values = spread * jax.random.normal(jax.random.fold_in(key, 23), (D, HEADS * HD), jnp.float32)
    stacked = jnp.stack([queries, key_part, values], axis=1)
    return jnp.clip(stacked, -0.19, 0.19).astype(jnp.bfloat16)


def draw_modulation(key, part):
    shift = 0.3 * jax.random.normal(jax.random.fold_in(key, 31), (NSTEP, D), jnp.float32)
    stretch = 0.3 * jax.random.normal(jax.random.fold_in(key, 32), (NSTEP, D), jnp.float32)
    gating = jax.random.normal(jax.random.fold_in(key, 33), (NSTEP, D), jnp.float32)
    return jnp.clip(jnp.stack([shift, stretch, gating], axis=1), -2.9, 2.9)


def draw_visible(key, part):
    coins = jax.random.randint(jax.random.fold_in(key, 41), (NCHUNK, NCHUNK), 0, 4)
    row_ids = jnp.arange(NCHUNK, dtype=jnp.int32)[:, None]
    col_ids = jnp.arange(NCHUNK, dtype=jnp.int32)[None, :]
    lower = jnp.where((coins > 0) & (row_ids > col_ids), 1, 0)
    return jnp.where(row_ids == col_ids, 1, lower).astype(jnp.int32)


def with_ends(result, rng, low, high):
    longest = result.shape.index(max(result.shape))
    spots = []
    for shift in (0, 1):
        where = [jax.random.randint(jax.random.fold_in(rng, axis), (), 0, length) for axis, length in enumerate(result.shape)]
        where[longest] = (where[longest] + shift) % result.shape[longest]
        spots.append(tuple(where))
    return result.at[spots[0]].set(low).at[spots[1]].set(high)


def block_scale(stream_key, dims, shards, least, top_value):
    gain = 1.0
    for dim, parts in shards:
        draws = jax.random.uniform(jax.random.fold_in(jax.random.fold_in(stream_key, 6), dim), (parts,), jnp.float32, least / len(shards), top_value / len(shards))
        gain = gain * jnp.repeat(jnp.exp(draws), dims[dim] // parts).reshape((-1,) + (1,) * (len(dims) - 1 - dim))
    return gain


def bell_draw(own_key, extent, deviation, bound, pieces=(), held_as=jnp.bfloat16):
    level = block_scale(own_key, extent, pieces, -0.22, 0.18) if pieces else 1.0
    array = jax.random.normal(own_key, extent, jnp.float32) * deviation * level
    return jnp.minimum(jnp.maximum(array, -bound), bound).astype(held_as)


def setup_inputs(seed: int = 0, part: int = 0) -> dict:
    splits = jax.random.split(jax.random.key(seed), 7)
    own_keys = jax.random.split(jax.random.fold_in(splits[6], part), 7)
    return {
        "frames": draw_frames(jax.random.fold_in(jax.random.fold_in(splits[6], part), 71), part),
        "levels": with_ends(jax.random.randint(own_keys[1], (NCHUNK,), 0, NSTEP), jax.random.fold_in(own_keys[1], 1), 0, NSTEP - 1).astype(jnp.int32),
        "visible": draw_visible(jax.random.fold_in(jax.random.fold_in(splits[6], part), 71), part),
        "w_qkv": draw_w_qkv(jax.random.fold_in(splits[6], 71), part),
        "w_out": bell_draw(splits[4], (HEADS * HD, D), (HEADS * HD // 64) ** -0.5, 1.5, ((0, 4),)),
        "modulation": draw_modulation(jax.random.fold_in(splits[6], 71), part),
    }


def reference(frames, levels, visible, w_qkv, w_out, modulation):
    styles = modulation[levels]
    floats = frames.astype(jnp.float32)
    normed = floats * lax.rsqrt(lax.optimization_barrier(jnp.mean(floats * floats, axis=-1, keepdims=True)) + 1e-06)
    shaped = (normed * (1.0 + styles[:, 1][:, None, :]) + styles[:, 0][:, None, :]).astype(jnp.bfloat16)
    qkv = jnp.dot(shaped.reshape(NCHUNK * CT, D), w_qkv.reshape(D, 3 * HEADS * HD), preferred_element_type=jnp.float32)
    qkv = qkv.astype(jnp.bfloat16).reshape(NCHUNK, CT, 3, HEADS, HD)
    queries = qkv[:, :, 0].astype(jnp.float32)
    key_rows = qkv[:, :, 1].astype(jnp.float32)
    values = qkv[:, :, 2].astype(jnp.float32)
    score_scale = HD ** (-0.5)

    def attend(inputs):
        query_block, visible_row = inputs
        scores = jnp.einsum('qhd,nkhd->qhnk', query_block, key_rows, precision=lax.Precision.HIGHEST) * score_scale
        allowed = (visible_row > 0)[None, None, :, None]
        scores = jnp.where(allowed, scores, -1e+30)
        row_peak = lax.optimization_barrier(jnp.max(scores, axis=(2, 3), keepdims=True))
        probs = jnp.where(allowed, jnp.exp(scores - row_peak), 0.0)
        denominator = lax.optimization_barrier(jnp.sum(probs, axis=(2, 3)))
        rounded = lax.optimization_barrier(probs.astype(jnp.bfloat16)).astype(jnp.float32)
        weighted = jnp.einsum('qhnk,nkhd->qhd', rounded, values, precision=lax.Precision.HIGHEST)
        return (weighted / denominator[:, :, None]).astype(jnp.bfloat16)
    attended = lax.map(attend, (queries, visible))
    flat = attended.reshape(NCHUNK * CT, HEADS * HD)
    span = H_DEV * HD

    def add_group(group, running):
        cols = lax.dynamic_slice_in_dim(flat, group * span, span, 1)
        rows = lax.dynamic_slice_in_dim(w_out, group * span, span, 0)
        partial_value = jnp.dot(cols, rows, preferred_element_type=jnp.float32)
        return running + lax.optimization_barrier(partial_value.astype(jnp.bfloat16)).astype(jnp.float32)
    summed = lax.fori_loop(0, N_HEAD, add_group, jnp.zeros((NCHUNK * CT, D), jnp.float32))
    summed = summed.reshape(NCHUNK, CT, D)
    return (summed * styles[:, 2][:, None, :]).astype(jnp.bfloat16)
```

```python
import functools

import jax
import jax.numpy as jnp
from jax import lax
from jax.experimental import pallas as pl
from jax.experimental.pallas import tpu as pltpu
from jax.sharding import PartitionSpec as P

HD = 128
PLANE = ("rep", "tract")


def from_behind(value, axis, by):
    count = lax.axis_size(axis)
    pairs = [(i, i + by) for i in range(count) if 0 <= i + by < count]
    return lax.ppermute(value, axis, pairs)


def pick_styles(levels, modulation):
    n_levels = modulation.shape[0]
    chosen = (lax.iota(jnp.int32, n_levels) == levels[0]).astype(jnp.float32)
    return jnp.tensordot(chosen, modulation, axes=1, precision=lax.Precision.HIGHEST)


def attention_kernel(heads_here, q_ref, *refs):
    kv_refs, seen_ref, out_ref = refs[:-2], refs[-2], refs[-1]
    cols = heads_here * HD
    score_scale = HD ** (-0.5)
    for h in range(heads_here):
        q = q_ref[:, h * HD : (h + 1) * HD]
        scores = []
        for d, kv in enumerate(kv_refs):
            raw = lax.dot_general(
                q,
                kv[:, h * HD : (h + 1) * HD],
                (((1,), (1,)), ((), ())),
                preferred_element_type=jnp.float32,
            )
            scores.append(jnp.where(seen_ref[d // 2] > 0, raw * score_scale, -1e30))
        peak = jnp.max(scores[0], axis=1, keepdims=True)
        for part in scores[1:]:
            peak = jnp.maximum(peak, jnp.max(part, axis=1, keepdims=True))
        denominator = jnp.zeros_like(peak)
        total = jnp.zeros((q.shape[0], HD), jnp.float32)
        for part, kv in zip(scores, kv_refs):
            probs = jnp.exp(part - peak)
            denominator += jnp.sum(probs, axis=1, keepdims=True)
            total += jnp.dot(
                probs.astype(jnp.bfloat16),
                kv[:, cols + h * HD : cols + (h + 1) * HD],
                preferred_element_type=jnp.float32,
            )
        out_ref[:, h * HD : (h + 1) * HD] = (total / denominator).astype(jnp.bfloat16)


def attend(queries, kv, seen):
    rows, cols = queries.shape
    vmem = pl.BlockSpec(memory_space=pltpu.VMEM)
    return pl.pallas_call(
        functools.partial(attention_kernel, cols // HD),
        out_shape=jax.ShapeDtypeStruct((rows, cols), jnp.bfloat16),
        in_specs=[vmem] * (1 + len(kv)) + [pl.BlockSpec(memory_space=pltpu.SMEM)],
        out_specs=vmem,
        compiler_params=pltpu.CompilerParams(vmem_limit_bytes=32 << 20),
        cost_estimate=pl.CostEstimate(
            flops=2 * rows * rows * len(kv) * cols,
            bytes_accessed=2 * rows * cols * (2 + len(kv)),
            transcendentals=rows * rows * len(kv) * cols // (2 * HD),
        ),
        name="attend",
    )(queries, *kv, seen)


def qkv_kernel(groups, outer_ref, *refs):
    count = sum(groups)
    tokens, w_ref, out_ref, rows_ref, acc_ref = refs[:count], *refs[count:]
    rows = tokens[0].shape[0]
    cols = w_ref.shape[2]
    step = pl.program_id(0)
    at = 0
    for i, size in enumerate(groups):
        block = tokens[at][...]
        if size == 2:
            block = jnp.where(outer_ref[0] > 0, block, tokens[at + 1][...])
        rows_ref[i * rows : (i + 1) * rows] = block
        at += size

    @pl.when(step == 0)
    def _():
        acc_ref[...] = jnp.zeros_like(acc_ref)

    for j in range(3):
        acc_ref[:, j * cols : (j + 1) * cols] += jnp.dot(
            rows_ref[...], w_ref[j], preferred_element_type=jnp.float32
        )

    @pl.when(step == pl.num_programs(0) - 1)
    def _():
        out_ref[...] = acc_ref[...].astype(out_ref.dtype)


def project_qkv(outer, groups, weights, chunk):
    tokens = [block for group in groups for block in group]
    rows, width = tokens[0].shape
    cols = weights.shape[2]
    total = rows * len(groups)
    return pl.pallas_call(
        functools.partial(qkv_kernel, [len(group) for group in groups]),
        grid=(width // chunk,),
        out_shape=jax.ShapeDtypeStruct((total, 3 * cols), jnp.bfloat16),
        in_specs=[pl.BlockSpec(memory_space=pltpu.SMEM)]
        + [pl.BlockSpec((rows, chunk), lambda k: (0, k))] * len(tokens)
        + [pl.BlockSpec((3, chunk, cols), lambda k: (0, k, 0))],
        out_specs=pl.BlockSpec((total, 3 * cols), lambda k: (0, 0)),
        scratch_shapes=[
            pltpu.VMEM((total, chunk), jnp.bfloat16),
            pltpu.VMEM((total, 3 * cols), jnp.float32),
        ],
        compiler_params=pltpu.CompilerParams(
            dimension_semantics=("arbitrary",), vmem_limit_bytes=32 << 20
        ),
        cost_estimate=pl.CostEstimate(
            flops=6 * total * width * cols,
            bytes_accessed=6 * width * cols + 2 * total * width,
            transcendentals=0,
        ),
        name="project_qkv",
    )(outer, *tokens, weights)


def output_kernel(place_ref, att_ref, gate_ref, own_ref, *refs):
    pieces, out_ref = refs[:-1], refs[-1]
    count = len(pieces) // 3
    span = out_ref.shape[1] // count
    width = own_ref.shape[0]
    rows = out_ref.shape[0] // 2
    core, chip = place_ref[0] % 2, place_ref[0] // 2
    for delta in range(count):
        chunk = chip ^ delta
        start = pl.multiple_of((core * count + chunk) * span, 128)
        there = pl.ds(start, span)
        total = jnp.dot(att_ref[:, :width], own_ref[:, there], preferred_element_type=jnp.float32)
        for s in range(3):
            total += jnp.dot(
                att_ref[:, (s + 1) * width : (s + 2) * width],
                pieces[count * s + delta][...],
                preferred_element_type=jnp.float32,
            )
        target = pl.ds(pl.multiple_of(chunk * span, 128), span)
        for half in range(2):
            part = total[half * rows : (half + 1) * rows] * gate_ref[half : half + 1, there]
            out_ref[half * rows : (half + 1) * rows, target] = part.astype(jnp.bfloat16)


def project_out(place, att, gate, own, pieces):
    rows, width = att.shape[0], own.shape[1] // 2
    vmem = pl.BlockSpec(memory_space=pltpu.VMEM)
    return pl.pallas_call(
        output_kernel,
        out_shape=jax.ShapeDtypeStruct((rows, width), jnp.bfloat16),
        in_specs=[pl.BlockSpec(memory_space=pltpu.SMEM)] + [vmem] * (3 + len(pieces)),
        out_specs=vmem,
        compiler_params=pltpu.CompilerParams(vmem_limit_bytes=40 << 20),
        cost_estimate=pl.CostEstimate(
            flops=2 * rows * att.shape[1] * width,
            bytes_accessed=2 * att.shape[1] * width,
            transcendentals=0,
        ),
        name="project_out",
    )(place, att, gate, own, *pieces)


def after(value, *earlier):
    return lax.optimization_barrier((value, *earlier))[0]


def gather_body(frames, levels, visible, w_qkv, w_out, modulation):
    here = lax.axis_index("head")
    n_tract = lax.axis_size("tract")
    tract = lax.axis_index("tract")
    plane = lax.axis_size("rep") * n_tract
    place = lax.axis_index("rep") * n_tract + tract
    core = lax.rem(place, 2)
    rows, width = frames.shape[1], frames.shape[2]
    cols = w_qkv.shape[2]
    span = width // plane
    outer = (here == 0) | (here == 3)
    outer_flag = outer.astype(jnp.int32)[None]
    w3 = jnp.moveaxis(w_qkv, 1, 0)

    def pair(value):
        return lax.ppermute(value, "head", [(0, 1), (1, 0), (2, 3), (3, 2)])

    def middle(value):
        return lax.ppermute(value, "head", [(1, 2), (2, 1)])

    def outward(value):
        return lax.ppermute(value, "head", [(1, 0), (2, 3)])

    def swap(value):
        return lax.ppermute(value, PLANE, [(i, i ^ 1) for i in range(plane)])

    def across_plane(piece):
        return [piece] + [
            lax.ppermute(piece, PLANE, [(i, i ^ delta) for i in range(plane)])
            for delta in range(2, plane, 2)
        ]

    chunk = core * (plane // 2) + place // 2
    piece = lax.dynamic_slice_in_dim(w_out, chunk * span, span, 1)
    w_first = pair(piece)
    w_mid = middle(piece)

    styles = lax.dynamic_index_in_dim(modulation, levels[0], 0, keepdims=False)
    floats = frames[0].astype(jnp.float32)
    normed = floats * lax.rsqrt(jnp.mean(floats * floats, axis=-1, keepdims=True) + 1e-06)
    own = (normed * (1.0 + styles[1]) + styles[0]).astype(jnp.bfloat16)

    ready = after(own, w_first, w_mid)
    first = pair(ready)
    mid = middle(ready)
    w_far_mid = middle(w_first)
    w_out_mid = outward(w_mid)
    w_far_out = outward(w_far_mid)
    w_first_pieces = across_plane(w_first)
    w_second = jnp.where(outer, w_out_mid, w_mid)
    w_second_pieces = across_plane(w_second)
    w_third = jnp.where(outer, w_far_out, w_far_mid)
    w_third_pieces = across_plane(w_third)
    far_mid = middle(after(first, w_out_mid, *w_first_pieces))
    out = outward(mid)
    far_out = outward(after(far_mid, *w_second_pieces))
    pieces = w_first_pieces + w_second_pieces + w_third_pieces
    gates = jnp.stack([styles[2], swap(styles[2])])

    def exchange(value):
        return [value] + [from_behind(value, "tract", d) for d in range(1, n_tract)]

    early = project_qkv(outer_flag, [[own], [first], [out, mid]], w3, 768)
    early_kv = exchange(early[:, cols:])
    late = project_qkv(outer_flag, [[after(far_out, *w_third_pieces), far_mid]], w3, 768)
    late_kv = exchange(late[:, cols:])
    kv = [block for both in zip(early_kv, late_kv) for block in both]
    offsets = tract - lax.iota(jnp.int32, n_tract)
    seen = jnp.sum(
        jnp.where(offsets[:, None] == lax.iota(jnp.int32, n_tract)[None, :], visible, 0), axis=1
    )
    queries = jnp.concatenate([early[:, :cols], late[:, :cols]], axis=0)
    attended = attend(queries, kv, seen)

    blocks = [attended[i * rows : (i + 1) * rows] for i in range(4)]
    leaving = [blocks[1], jnp.where(outer, blocks[2], blocks[3]), jnp.where(outer, blocks[3], blocks[2])]
    came = [
        lax.ppermute(value, "head", [(i, i ^ (s + 1)) for i in range(4)])
        for s, value in enumerate(leaving)
    ]
    att = jnp.concatenate(
        [blocks[0], came[0], jnp.where(outer, came[1], came[2]), jnp.where(outer, came[2], came[1])],
        axis=1,
    )
    both = project_out(place[None], jnp.concatenate([att, swap(att)], axis=0), gates, w_out, pieces)
    mine, theirs = both[:rows], swap(both[rows:])
    mixed = jnp.where(
        core == 0,
        jnp.concatenate([mine, theirs], axis=1),
        jnp.concatenate([theirs, mine], axis=1),
    )
    return mixed[None]


def scatter_body(frames, levels, visible, w_qkv, w_out, modulation):
    col_width = w_qkv.shape[2]
    heads_here = col_width // HD
    styles = pick_styles(levels, modulation)
    floats = lax.all_gather(frames, "head", axis=1, tiled=True).astype(jnp.float32)
    normed = floats * lax.rsqrt(jnp.mean(floats * floats, axis=-1, keepdims=True) + 1e-06)
    shaped = (normed * (1.0 + styles[1]) + styles[0]).astype(jnp.bfloat16)
    qkv = jnp.einsum("crd,dke->crke", shaped, w_qkv, preferred_element_type=jnp.float32).astype(
        jnp.bfloat16
    )
    total_rows = qkv.shape[1]
    queries = qkv[0, :, 0].reshape(total_rows, heads_here, HD)
    kv_block = qkv[:, :, 1:]
    visible_row = visible[0]
    score_scale = HD ** (-0.5)

    def absorb(state, incoming, offset):
        row_peak, denominator, running = state
        blocks = incoming.shape[0]
        allowed = (lax.dynamic_slice_in_dim(visible_row, offset, blocks) > 0) & (offset >= 0)
        key_rows = incoming[:, :, 0].reshape(blocks, total_rows, heads_here, HD)
        values = incoming[:, :, 1].reshape(blocks, total_rows, heads_here, HD)
        scores = (
            jnp.einsum("qhd,nkhd->qhnk", queries, key_rows, preferred_element_type=jnp.float32)
            * score_scale
        )
        allowed = allowed[None, None, :, None]
        scores = jnp.where(allowed, scores, -1e30)
        new_peak = jnp.maximum(row_peak, jnp.max(scores, axis=(2, 3)))
        probs = jnp.where(allowed, jnp.exp(scores - new_peak[:, :, None, None]), 0.0)
        rescale = jnp.exp(row_peak - new_peak)
        denominator = denominator * rescale + jnp.sum(probs, axis=(2, 3))
        weighted = jnp.einsum(
            "qhnk,nkhd->qhd", probs.astype(jnp.bfloat16), values, preferred_element_type=jnp.float32
        )
        running = running * rescale[:, :, None] + weighted
        return (new_peak, denominator, running)

    initial = (
        jnp.full((total_rows, heads_here), -1e30, jnp.float32),
        jnp.zeros((total_rows, heads_here), jnp.float32),
        jnp.zeros((total_rows, heads_here, HD), jnp.float32),
    )
    own_index = lax.axis_index("tract")
    state = absorb(initial, kv_block, own_index)
    for distance in range(1, lax.axis_size("tract")):
        moved = from_behind(kv_block, "tract", distance)
        state = absorb(state, moved, own_index - distance)
    row_peak, denominator, running = state
    attended = (
        (running / denominator[:, :, None]).astype(jnp.bfloat16).reshape(total_rows, col_width)
    )
    summed = lax.psum_scatter(
        jnp.dot(attended, w_out, preferred_element_type=jnp.float32).astype(jnp.bfloat16),
        "head",
        scatter_dimension=0,
        tiled=True,
    ).astype(jnp.float32)
    mixed = (summed * styles[2]).astype(jnp.bfloat16)
    return mixed[None]


def solution(mesh):
    placed = (
        P(("rep", "tract"), "head", None),
        P(("rep", "tract")),
        P(("rep", "tract"), None),
        P(None, None, "head"),
        P("head", None),
        P(),
    )

    def run(frames, levels, visible, w_qkv, w_out, modulation):
        n_head, n_tract, n_rep = mesh.shape["head"], mesh.shape["tract"], mesh.shape["rep"]
        tokens_here = frames.shape[1] // n_head
        weight_rows_here = w_out.shape[0] // n_head
        plane = n_tract * n_rep
        fits = (n_head, n_tract, n_rep) == (4, 4, 2) and frames.shape[2] % (2 * plane * 128) == 0
        gather = fits and weight_rows_here < tokens_here * plane
        return jax.shard_map(
            gather_body if gather else scatter_body,
            mesh=mesh,
            in_specs=placed,
            out_specs=P(("rep", "tract"), "head", None),
            check_vma=False,
        )(frames, levels, visible, w_qkv, w_out, modulation)

    return run
```

```python
import functools

import jax
import jax.numpy as jnp
from jax import lax
from jax.experimental import pallas as pl
from jax.experimental.pallas import tpu as pltpu
from jax.sharding import PartitionSpec as P

HD = 128
PLANE = ("rep", "tract")


def from_behind(value, axis, by):
    count = lax.axis_size(axis)
    pairs = [(i, i + by) for i in range(count) if 0 <= i + by < count]
    return lax.ppermute(value, axis, pairs)


def pick_styles(levels, modulation):
    n_levels = modulation.shape[0]
    chosen = (lax.iota(jnp.int32, n_levels) == levels[0]).astype(jnp.float32)
    return jnp.tensordot(chosen, modulation, axes=1, precision=lax.Precision.HIGHEST)


def attention_kernel(heads_here, q_ref, *refs):
    kv_refs, seen_ref, out_ref = refs[:-2], refs[-2], refs[-1]
    cols = heads_here * HD
    score_scale = HD ** (-0.5)
    for h in range(heads_here):
        q = q_ref[:, h * HD : (h + 1) * HD]
        scores = []
        for d, kv in enumerate(kv_refs):
            raw = lax.dot_general(
                q,
                kv[:, h * HD : (h + 1) * HD],
                (((1,), (1,)), ((), ())),
                preferred_element_type=jnp.float32,
            )
            scores.append(jnp.where(seen_ref[d] > 0, raw * score_scale, -1e30))
        peak = jnp.max(scores[0], axis=1, keepdims=True)
        for part in scores[1:]:
            peak = jnp.maximum(peak, jnp.max(part, axis=1, keepdims=True))
        denominator = jnp.zeros_like(peak)
        total = jnp.zeros((q.shape[0], HD), jnp.float32)
        for part, kv in zip(scores, kv_refs):
            probs = jnp.exp(part - peak)
            denominator += jnp.sum(probs, axis=1, keepdims=True)
            total += jnp.dot(
                probs.astype(jnp.bfloat16),
                kv[:, cols + h * HD : cols + (h + 1) * HD],
                preferred_element_type=jnp.float32,
            )
        out_ref[:, h * HD : (h + 1) * HD] = (total / denominator).astype(jnp.bfloat16)


def attend(queries, kv, seen):
    rows, cols = queries.shape
    vmem = pl.BlockSpec(memory_space=pltpu.VMEM)
    return pl.pallas_call(
        functools.partial(attention_kernel, cols // HD),
        out_shape=jax.ShapeDtypeStruct((rows, cols), jnp.bfloat16),
        in_specs=[vmem] * (1 + len(kv)) + [pl.BlockSpec(memory_space=pltpu.SMEM)],
        out_specs=vmem,
        compiler_params=pltpu.CompilerParams(vmem_limit_bytes=32 << 20),
        cost_estimate=pl.CostEstimate(
            flops=2 * rows * rows * len(kv) * cols,
            bytes_accessed=2 * rows * cols * (2 + len(kv)),
            transcendentals=rows * rows * len(kv) * cols // (2 * HD),
        ),
        name="attend",
    )(queries, *kv, seen)


def shape_kernel(level_ref, frames_ref, style_ref, out_ref, gate_ref):
    count, _, span = out_ref.shape
    floats = frames_ref[...].astype(jnp.float32)
    scale = lax.rsqrt(jnp.mean(floats * floats, axis=-1, keepdims=True) + 1e-06)
    for c in range(count):
        part = slice(c * span, (c + 1) * span)
        normed = frames_ref[:, part].astype(jnp.float32) * scale
        shaped = normed * (1.0 + style_ref[0, 1:2, part]) + style_ref[0, 0:1, part]
        out_ref[c] = shaped.astype(jnp.bfloat16)
    gate_ref[...] = style_ref[0, 2:3]


def shape_tokens(levels, frames, modulation, count):
    rows, width = frames.shape
    span = width // count
    blocks, gate = pl.pallas_call(
        shape_kernel,
        grid_spec=pltpu.PrefetchScalarGridSpec(
            num_scalar_prefetch=1,
            grid=(1,),
            in_specs=[
                pl.BlockSpec((rows, width), lambda i, level: (0, 0)),
                pl.BlockSpec((1,) + modulation.shape[1:], lambda i, level: (level[0], 0, 0)),
            ],
            out_specs=[
                pl.BlockSpec((count, rows, span), lambda i, level: (0, 0, 0)),
                pl.BlockSpec((1, width), lambda i, level: (0, 0)),
            ],
        ),
        out_shape=[
            jax.ShapeDtypeStruct((count, rows, span), jnp.bfloat16),
            jax.ShapeDtypeStruct((1, width), jnp.float32),
        ],
        compiler_params=pltpu.CompilerParams(vmem_limit_bytes=32 << 20),
        cost_estimate=pl.CostEstimate(
            flops=6 * rows * width, bytes_accessed=4 * rows * width, transcendentals=rows
        ),
        name="shape_tokens",
    )(levels, frames, modulation)
    return blocks.reshape(count * rows, span), gate


def qkv_kernel(groups, outer_ref, *refs):
    count = sum(groups)
    tokens, w_ref, out_ref, rows_ref = refs[:count], *refs[count:]
    cols = w_ref.shape[2]
    chunk = rows_ref.shape[1]
    rows = rows_ref.shape[0] // len(groups)
    total = [jnp.zeros((rows_ref.shape[0], cols), jnp.float32) for _ in range(3)]
    for k in range(w_ref.shape[1] // chunk):
        at = 0
        source = slice(k * rows, (k + 1) * rows)
        for i, size in enumerate(groups):
            block = tokens[at][source]
            if size == 2:
                block = jnp.where(outer_ref[0] > 0, block, tokens[at + 1][source])
            rows_ref[i * rows : (i + 1) * rows] = block
            at += size
        for j in range(3):
            total[j] += jnp.dot(
                rows_ref[...],
                w_ref[j, k * chunk : (k + 1) * chunk],
                preferred_element_type=jnp.float32,
            )
    for j in range(3):
        out_ref[:, j * cols : (j + 1) * cols] = total[j].astype(out_ref.dtype)


def project_qkv(outer, groups, weights, rows):
    tokens = [block for group in groups for block in group]
    chunk = tokens[0].shape[1]
    width, cols = weights.shape[1], weights.shape[2]
    total = rows * len(groups)
    vmem = pl.BlockSpec(memory_space=pltpu.VMEM)
    return pl.pallas_call(
        functools.partial(qkv_kernel, [len(group) for group in groups]),
        out_shape=jax.ShapeDtypeStruct((total, 3 * cols), jnp.bfloat16),
        in_specs=[pl.BlockSpec(memory_space=pltpu.SMEM)] + [vmem] * (len(tokens) + 1),
        out_specs=vmem,
        scratch_shapes=[pltpu.VMEM((total, chunk), jnp.bfloat16)],
        compiler_params=pltpu.CompilerParams(vmem_limit_bytes=40 << 20),
        cost_estimate=pl.CostEstimate(
            flops=6 * total * width * cols,
            bytes_accessed=6 * width * cols + 2 * total * width,
            transcendentals=0,
        ),
        name="project_qkv",
    )(outer, *tokens, weights)


def output_kernel(place_ref, att_ref, gate_ref, own_ref, *refs):
    pieces, out_ref = refs[:-1], refs[-1]
    count = len(pieces) // 3
    span = out_ref.shape[1] // count
    width = own_ref.shape[0]
    rows = out_ref.shape[0] // 2
    core, chip = place_ref[0] % 2, place_ref[0] // 2
    for delta in range(count):
        chunk = chip ^ delta
        start = pl.multiple_of((core * count + chunk) * span, 128)
        there = pl.ds(start, span)
        total = jnp.dot(att_ref[:, :width], own_ref[:, there], preferred_element_type=jnp.float32)
        for s in range(3):
            total += jnp.dot(
                att_ref[:, (s + 1) * width : (s + 2) * width],
                pieces[count * s + delta][...],
                preferred_element_type=jnp.float32,
            )
        target = pl.ds(pl.multiple_of(chunk * span, 128), span)
        for half in range(2):
            part = total[half * rows : (half + 1) * rows] * gate_ref[half : half + 1, there]
            out_ref[half * rows : (half + 1) * rows, target] = part.astype(jnp.bfloat16)


def project_out(place, att, gate, own, pieces):
    rows, width = att.shape[0], own.shape[1] // 2
    vmem = pl.BlockSpec(memory_space=pltpu.VMEM)
    return pl.pallas_call(
        output_kernel,
        out_shape=jax.ShapeDtypeStruct((rows, width), jnp.bfloat16),
        in_specs=[pl.BlockSpec(memory_space=pltpu.SMEM)] + [vmem] * (3 + len(pieces)),
        out_specs=vmem,
        compiler_params=pltpu.CompilerParams(vmem_limit_bytes=40 << 20),
        cost_estimate=pl.CostEstimate(
            flops=2 * rows * att.shape[1] * width,
            bytes_accessed=2 * att.shape[1] * width,
            transcendentals=0,
        ),
        name="project_out",
    )(place, att, gate, own, *pieces)


def after(value, *earlier):
    return lax.optimization_barrier((value, *earlier))[0]


def gather_body(frames, levels, visible, w_qkv, w_out, modulation):
    here = lax.axis_index("head")
    n_tract = lax.axis_size("tract")
    tract = lax.axis_index("tract")
    plane = lax.axis_size("rep") * n_tract
    place = lax.axis_index("rep") * n_tract + tract
    core = lax.rem(place, 2)
    rows, width = frames.shape[1], frames.shape[2]
    cols = w_qkv.shape[2]
    span = width // plane
    outer = (here == 0) | (here == 3)
    outer_flag = outer.astype(jnp.int32)[None]
    w3 = jnp.moveaxis(w_qkv, 1, 0)

    def pair(value):
        return lax.ppermute(value, "head", [(0, 1), (1, 0), (2, 3), (3, 2)])

    def middle(value):
        return lax.ppermute(value, "head", [(1, 2), (2, 1)])

    def outward(value):
        return lax.ppermute(value, "head", [(1, 0), (2, 3)])

    def swap(value):
        return lax.ppermute(value, PLANE, [(i, i ^ 1) for i in range(plane)])

    def across_plane(piece):
        return [piece] + [
            lax.ppermute(piece, PLANE, [(i, i ^ delta) for i in range(plane)])
            for delta in range(2, plane, 2)
        ]

    chunk = core * (plane // 2) + place // 2
    piece = lax.dynamic_slice_in_dim(w_out, chunk * span, span, 1)
    w_first = pair(piece)
    w_mid = middle(piece)
    own, gate = shape_tokens(levels, frames[0], modulation, plane)
    gates = jnp.concatenate([gate, swap(gate)], axis=0)
    high = own.shape[0]

    first = pair(after(jnp.concatenate([own, w_mid], axis=0), gates))
    mid = middle(jnp.concatenate([own, w_first], axis=0))
    w_first_pieces = across_plane(w_first)
    far_mid = middle(after(first[:high], *w_first_pieces))
    out = outward(mid)
    w_second_pieces = across_plane(jnp.where(outer, first[high:], w_mid))
    far_out = outward(after(far_mid, out, *w_second_pieces))
    w_third_pieces = across_plane(jnp.where(outer, out[high:], mid[high:]))
    pieces = w_first_pieces + w_second_pieces + w_third_pieces

    early = project_qkv(outer_flag, [[own], [first], [out, mid]], w3, rows)
    late = project_qkv(outer_flag, [[far_out, far_mid]], w3, rows)
    qkv = jnp.concatenate([early, late], axis=0)
    kv_own = qkv[:, cols:]
    kv = [kv_own] + [from_behind(kv_own, "tract", d) for d in range(1, n_tract)]
    offsets = tract - lax.iota(jnp.int32, n_tract)
    seen = jnp.sum(
        jnp.where(offsets[:, None] == lax.iota(jnp.int32, n_tract)[None, :], visible, 0), axis=1
    )
    attended = attend(after(qkv[:, :cols], *w_third_pieces), kv, seen)

    blocks = [attended[i * rows : (i + 1) * rows] for i in range(4)]
    leaving = [blocks[1], jnp.where(outer, blocks[2], blocks[3]), jnp.where(outer, blocks[3], blocks[2])]
    came = [
        lax.ppermute(value, "head", [(i, i ^ (s + 1)) for i in range(4)])
        for s, value in enumerate(leaving)
    ]
    att = jnp.concatenate(
        [blocks[0], came[0], jnp.where(outer, came[1], came[2]), jnp.where(outer, came[2], came[1])],
        axis=1,
    )
    both = project_out(place[None], jnp.concatenate([att, swap(att)], axis=0), gates, w_out, pieces)
    mine, theirs = both[:rows], swap(both[rows:])
    mixed = jnp.where(
        core == 0,
        jnp.concatenate([mine, theirs], axis=1),
        jnp.concatenate([theirs, mine], axis=1),
    )
    return mixed[None]


def scatter_body(frames, levels, visible, w_qkv, w_out, modulation):
    col_width = w_qkv.shape[2]
    heads_here = col_width // HD
    styles = pick_styles(levels, modulation)
    floats = lax.all_gather(frames, "head", axis=1, tiled=True).astype(jnp.float32)
    normed = floats * lax.rsqrt(jnp.mean(floats * floats, axis=-1, keepdims=True) + 1e-06)
    shaped = (normed * (1.0 + styles[1]) + styles[0]).astype(jnp.bfloat16)
    qkv = jnp.einsum("crd,dke->crke", shaped, w_qkv, preferred_element_type=jnp.float32).astype(
        jnp.bfloat16
    )
    total_rows = qkv.shape[1]
    queries = qkv[0, :, 0].reshape(total_rows, heads_here, HD)
    kv_block = qkv[:, :, 1:]
    visible_row = visible[0]
    score_scale = HD ** (-0.5)

    def absorb(state, incoming, offset):
        row_peak, denominator, running = state
        blocks = incoming.shape[0]
        allowed = (lax.dynamic_slice_in_dim(visible_row, offset, blocks) > 0) & (offset >= 0)
        key_rows = incoming[:, :, 0].reshape(blocks, total_rows, heads_here, HD)
        values = incoming[:, :, 1].reshape(blocks, total_rows, heads_here, HD)
        scores = (
            jnp.einsum("qhd,nkhd->qhnk", queries, key_rows, preferred_element_type=jnp.float32)
            * score_scale
        )
        allowed = allowed[None, None, :, None]
        scores = jnp.where(allowed, scores, -1e30)
        new_peak = jnp.maximum(row_peak, jnp.max(scores, axis=(2, 3)))
        probs = jnp.where(allowed, jnp.exp(scores - new_peak[:, :, None, None]), 0.0)
        rescale = jnp.exp(row_peak - new_peak)
        denominator = denominator * rescale + jnp.sum(probs, axis=(2, 3))
        weighted = jnp.einsum(
            "qhnk,nkhd->qhd", probs.astype(jnp.bfloat16), values, preferred_element_type=jnp.float32
        )
        running = running * rescale[:, :, None] + weighted
        return (new_peak, denominator, running)

    initial = (
        jnp.full((total_rows, heads_here), -1e30, jnp.float32),
        jnp.zeros((total_rows, heads_here), jnp.float32),
        jnp.zeros((total_rows, heads_here, HD), jnp.float32),
    )
    own_index = lax.axis_index("tract")
    state = absorb(initial, kv_block, own_index)
    for distance in range(1, lax.axis_size("tract")):
        moved = from_behind(kv_block, "tract", distance)
        state = absorb(state, moved, own_index - distance)
    row_peak, denominator, running = state
    attended = (
        (running / denominator[:, :, None]).astype(jnp.bfloat16).reshape(total_rows, col_width)
    )
    summed = lax.psum_scatter(
        jnp.dot(attended, w_out, preferred_element_type=jnp.float32).astype(jnp.bfloat16),
        "head",
        scatter_dimension=0,
        tiled=True,
    ).astype(jnp.float32)
    mixed = (summed * styles[2]).astype(jnp.bfloat16)
    return mixed[None]


def solution(mesh):
    placed = (
        P(("rep", "tract"), "head", None),
        P(("rep", "tract")),
        P(("rep", "tract"), None),
        P(None, None, "head"),
        P("head", None),
        P(),
    )

    def run(frames, levels, visible, w_qkv, w_out, modulation):
        n_head, n_tract, n_rep = mesh.shape["head"], mesh.shape["tract"], mesh.shape["rep"]
        tokens_here = frames.shape[1] // n_head
        weight_rows_here = w_out.shape[0] // n_head
        plane = n_tract * n_rep
        fits = (n_head, n_tract, n_rep) == (4, 4, 2) and frames.shape[2] % (2 * plane * 128) == 0
        gather = fits and weight_rows_here < tokens_here * plane
        return jax.shard_map(
            gather_body if gather else scatter_body,
            mesh=mesh,
            in_specs=placed,
            out_specs=P(("rep", "tract"), "head", None),
            check_vma=False,
        )(frames, levels, visible, w_qkv, w_out, modulation)

    return run
```

```python
import functools

import jax
import jax.numpy as jnp
from jax import lax
from jax.experimental import pallas as pl
from jax.experimental.pallas import tpu as pltpu
from jax.sharding import PartitionSpec as P

HD = 128
PLANE = ("rep", "tract")


def from_behind(value, axis, by):
    count = lax.axis_size(axis)
    pairs = [(i, i + by) for i in range(count) if 0 <= i + by < count]
    return lax.ppermute(value, axis, pairs)


def pick_styles(levels, modulation):
    n_levels = modulation.shape[0]
    chosen = (lax.iota(jnp.int32, n_levels) == levels[0]).astype(jnp.float32)
    return jnp.tensordot(chosen, modulation, axes=1, precision=lax.Precision.HIGHEST)


def attention_kernel(heads_here, q_ref, *refs):
    kv_refs, seen_ref, out_ref = refs[:-2], refs[-2], refs[-1]
    cols = heads_here * HD
    score_scale = HD ** (-0.5)
    for h in range(heads_here):
        q = q_ref[:, h * HD : (h + 1) * HD]
        scores = []
        for d, kv in enumerate(kv_refs):
            raw = lax.dot_general(
                q,
                kv[:, h * HD : (h + 1) * HD],
                (((1,), (1,)), ((), ())),
                preferred_element_type=jnp.float32,
            )
            scores.append(jnp.where(seen_ref[d] > 0, raw * score_scale, -1e30))
        peak = jnp.max(scores[0], axis=1, keepdims=True)
        for part in scores[1:]:
            peak = jnp.maximum(peak, jnp.max(part, axis=1, keepdims=True))
        denominator = jnp.zeros_like(peak)
        total = jnp.zeros((q.shape[0], HD), jnp.float32)
        for part, kv in zip(scores, kv_refs):
            probs = jnp.exp(part - peak)
            denominator += jnp.sum(probs, axis=1, keepdims=True)
            total += jnp.dot(
                probs.astype(jnp.bfloat16),
                kv[:, cols + h * HD : cols + (h + 1) * HD],
                preferred_element_type=jnp.float32,
            )
        out_ref[:, h * HD : (h + 1) * HD] = (total / denominator).astype(jnp.bfloat16)


def attend(queries, kv, seen):
    rows, cols = queries.shape
    vmem = pl.BlockSpec(memory_space=pltpu.VMEM)
    return pl.pallas_call(
        functools.partial(attention_kernel, cols // HD),
        out_shape=jax.ShapeDtypeStruct((rows, cols), jnp.bfloat16),
        in_specs=[vmem] * (1 + len(kv)) + [pl.BlockSpec(memory_space=pltpu.SMEM)],
        out_specs=vmem,
        compiler_params=pltpu.CompilerParams(vmem_limit_bytes=32 << 20),
        cost_estimate=pl.CostEstimate(
            flops=2 * rows * rows * len(kv) * cols,
            bytes_accessed=2 * rows * cols * (2 + len(kv)),
            transcendentals=rows * rows * len(kv) * cols // (2 * HD),
        ),
        name="attend",
    )(queries, *kv, seen)


def shape_kernel(level_ref, frames_ref, style_ref, out_ref, gate_ref):
    count, _, span = out_ref.shape
    floats = frames_ref[...].astype(jnp.float32)
    scale = lax.rsqrt(jnp.mean(floats * floats, axis=-1, keepdims=True) + 1e-06)
    for c in range(count):
        part = slice(c * span, (c + 1) * span)
        normed = frames_ref[:, part].astype(jnp.float32) * scale
        shaped = normed * (1.0 + style_ref[0, 1:2, part]) + style_ref[0, 0:1, part]
        out_ref[c] = shaped.astype(jnp.bfloat16)
    gate_ref[...] = style_ref[0, 2:3]


def shape_tokens(levels, frames, modulation, count):
    rows, width = frames.shape
    span = width // count
    blocks, gate = pl.pallas_call(
        shape_kernel,
        grid_spec=pltpu.PrefetchScalarGridSpec(
            num_scalar_prefetch=1,
            grid=(1,),
            in_specs=[
                pl.BlockSpec((rows, width), lambda i, level: (0, 0)),
                pl.BlockSpec((1,) + modulation.shape[1:], lambda i, level: (level[0], 0, 0)),
            ],
            out_specs=[
                pl.BlockSpec((count, rows, span), lambda i, level: (0, 0, 0)),
                pl.BlockSpec((1, width), lambda i, level: (0, 0)),
            ],
        ),
        out_shape=[
            jax.ShapeDtypeStruct((count, rows, span), jnp.bfloat16),
            jax.ShapeDtypeStruct((1, width), jnp.float32),
        ],
        compiler_params=pltpu.CompilerParams(vmem_limit_bytes=32 << 20),
        cost_estimate=pl.CostEstimate(
            flops=6 * rows * width, bytes_accessed=4 * rows * width, transcendentals=rows
        ),
        name="shape_tokens",
    )(levels, frames, modulation)
    return blocks.reshape(count * rows, span), gate


def qkv_kernel(groups, outer_ref, *refs):
    count = sum(groups)
    tokens, w_ref, out_ref, rows_ref = refs[:count], *refs[count:]
    cols = w_ref.shape[2]
    chunk = rows_ref.shape[1]
    rows = rows_ref.shape[0] // len(groups)
    total = [jnp.zeros((rows_ref.shape[0], cols), jnp.float32) for _ in range(3)]
    for k in range(w_ref.shape[1] // chunk):
        at = 0
        source = slice(k * rows, (k + 1) * rows)
        for i, size in enumerate(groups):
            block = tokens[at][source]
            if size == 2:
                block = jnp.where(outer_ref[0] > 0, block, tokens[at + 1][source])
            rows_ref[i * rows : (i + 1) * rows] = block
            at += size
        for j in range(3):
            total[j] += jnp.dot(
                rows_ref[...],
                w_ref[j, k * chunk : (k + 1) * chunk],
                preferred_element_type=jnp.float32,
            )
    for j in range(3):
        out_ref[:, j * cols : (j + 1) * cols] = total[j].astype(out_ref.dtype)


def project_qkv(outer, groups, weights, rows):
    tokens = [block for group in groups for block in group]
    chunk = tokens[0].shape[1]
    width, cols = weights.shape[1], weights.shape[2]
    total = rows * len(groups)
    vmem = pl.BlockSpec(memory_space=pltpu.VMEM)
    return pl.pallas_call(
        functools.partial(qkv_kernel, [len(group) for group in groups]),
        out_shape=jax.ShapeDtypeStruct((total, 3 * cols), jnp.bfloat16),
        in_specs=[pl.BlockSpec(memory_space=pltpu.SMEM)] + [vmem] * (len(tokens) + 1),
        out_specs=vmem,
        scratch_shapes=[pltpu.VMEM((total, chunk), jnp.bfloat16)],
        compiler_params=pltpu.CompilerParams(vmem_limit_bytes=40 << 20),
        cost_estimate=pl.CostEstimate(
            flops=6 * total * width * cols,
            bytes_accessed=6 * width * cols + 2 * total * width,
            transcendentals=0,
        ),
        name="project_qkv",
    )(outer, *tokens, weights)


def output_kernel(place_ref, att_ref, gate_ref, own_ref, *refs):
    pieces, out_ref = refs[:-1], refs[-1]
    count = len(pieces) // 3
    span = out_ref.shape[1] // count
    width = own_ref.shape[0]
    rows = out_ref.shape[0] // 2
    core, chip = place_ref[0] % 2, place_ref[0] // 2
    for delta in range(count):
        chunk = chip ^ delta
        start = pl.multiple_of((core * count + chunk) * span, 128)
        there = pl.ds(start, span)
        total = jnp.dot(att_ref[:, :width], own_ref[:, there], preferred_element_type=jnp.float32)
        for s in range(3):
            total += jnp.dot(
                att_ref[:, (s + 1) * width : (s + 2) * width],
                pieces[count * s + delta][...],
                preferred_element_type=jnp.float32,
            )
        target = pl.ds(pl.multiple_of(chunk * span, 128), span)
        for half in range(2):
            part = total[half * rows : (half + 1) * rows] * gate_ref[half : half + 1, there]
            out_ref[half * rows : (half + 1) * rows, target] = part.astype(jnp.bfloat16)


def project_out(place, att, gate, own, pieces):
    rows, width = att.shape[0], own.shape[1] // 2
    vmem = pl.BlockSpec(memory_space=pltpu.VMEM)
    return pl.pallas_call(
        output_kernel,
        out_shape=jax.ShapeDtypeStruct((rows, width), jnp.bfloat16),
        in_specs=[pl.BlockSpec(memory_space=pltpu.SMEM)] + [vmem] * (3 + len(pieces)),
        out_specs=vmem,
        compiler_params=pltpu.CompilerParams(vmem_limit_bytes=40 << 20),
        cost_estimate=pl.CostEstimate(
            flops=16 * rows * att.shape[1] * width,
            bytes_accessed=2 * rows * width,
            transcendentals=0,
        ),
        name="project_out",
    )(place, att, gate, own, *pieces)


def after(value, *earlier):
    return lax.optimization_barrier((value, *earlier))[0]


def gather_body(frames, levels, visible, w_qkv, w_out, modulation):
    here = lax.axis_index("head")
    n_tract = lax.axis_size("tract")
    tract = lax.axis_index("tract")
    plane = lax.axis_size("rep") * n_tract
    place = lax.axis_index("rep") * n_tract + tract
    core = lax.rem(place, 2)
    rows, width = frames.shape[1], frames.shape[2]
    cols = w_qkv.shape[2]
    span = width // plane
    outer = (here == 0) | (here == 3)
    outer_flag = outer.astype(jnp.int32)[None]
    w3 = jnp.moveaxis(w_qkv, 1, 0)

    def pair(value):
        return lax.ppermute(value, "head", [(0, 1), (1, 0), (2, 3), (3, 2)])

    def middle(value):
        return lax.ppermute(value, "head", [(1, 2), (2, 1)])

    def outward(value):
        return lax.ppermute(value, "head", [(1, 0), (2, 3)])

    def swap(value):
        return lax.ppermute(value, PLANE, [(i, i ^ 1) for i in range(plane)])

    def across_plane(piece):
        return [piece] + [
            lax.ppermute(piece, PLANE, [(i, i ^ delta) for i in range(plane)])
            for delta in range(2, plane, 2)
        ]

    chunk = core * (plane // 2) + place // 2
    piece = lax.dynamic_slice_in_dim(w_out, chunk * span, span, 1)
    w_first = pair(piece)
    w_mid = middle(piece)
    own, gate = shape_tokens(levels, frames[0], modulation, plane)
    gates = jnp.concatenate([gate, swap(gate)], axis=0)
    high = own.shape[0]

    first = pair(after(jnp.concatenate([own, w_mid], axis=0), gates))
    mid = middle(jnp.concatenate([own, w_first], axis=0))
    w_first_pieces = across_plane(w_first)
    far_mid = middle(after(first[:high], *w_first_pieces))
    out = outward(mid)
    w_second_pieces = across_plane(jnp.where(outer, first[high:], w_mid))
    far_out = outward(after(far_mid, out, *w_second_pieces))
    w_third_pieces = across_plane(jnp.where(outer, out[high:], mid[high:]))
    pieces = w_first_pieces + w_second_pieces + w_third_pieces

    early = project_qkv(outer_flag, [[own], [first], [out, mid]], w3, rows)
    late = project_qkv(outer_flag, [[far_out, far_mid]], w3, rows)
    qkv = jnp.concatenate([early, late], axis=0)
    kv_own = after(qkv[:, cols:], *w_third_pieces)
    kv_chip = from_behind(kv_own, "tract", 2)
    kv_core = lax.ppermute(kv_own, "tract", [(0, 1), (2, 3)])
    kv_both = lax.ppermute(kv_chip, "tract", [(2, 3), (3, 2)])
    sources = jnp.stack(
        [
            tract,
            jnp.where(tract % 2 == 1, tract - 1, -1),
            tract - 2,
            jnp.where(tract > 1, 3 - tract, -1),
        ]
    )
    seen = jnp.sum(
        jnp.where(sources[:, None] == lax.iota(jnp.int32, n_tract)[None, :], visible, 0), axis=1
    )
    attended = attend(
        qkv[:, :cols], [kv_own, kv_core, kv_chip, kv_both], seen
    )

    blocks = [attended[i * rows : (i + 1) * rows] for i in range(4)]
    leaving = [blocks[1], jnp.where(outer, blocks[2], blocks[3]), jnp.where(outer, blocks[3], blocks[2])]
    came = [
        lax.ppermute(value, "head", [(i, i ^ (s + 1)) for i in range(4)])
        for s, value in enumerate(leaving)
    ]
    att = jnp.concatenate(
        [blocks[0], came[0], jnp.where(outer, came[1], came[2]), jnp.where(outer, came[2], came[1])],
        axis=1,
    )
    both = project_out(place[None], jnp.concatenate([att, swap(att)], axis=0), gates, w_out, pieces)
    mine, theirs = both[:rows], swap(both[rows:])
    mixed = jnp.where(
        core == 0,
        jnp.concatenate([mine, theirs], axis=1),
        jnp.concatenate([theirs, mine], axis=1),
    )
    return mixed[None]


def scatter_body(frames, levels, visible, w_qkv, w_out, modulation):
    col_width = w_qkv.shape[2]
    heads_here = col_width // HD
    styles = pick_styles(levels, modulation)
    floats = lax.all_gather(frames, "head", axis=1, tiled=True).astype(jnp.float32)
    normed = floats * lax.rsqrt(jnp.mean(floats * floats, axis=-1, keepdims=True) + 1e-06)
    shaped = (normed * (1.0 + styles[1]) + styles[0]).astype(jnp.bfloat16)
    qkv = jnp.einsum("crd,dke->crke", shaped, w_qkv, preferred_element_type=jnp.float32).astype(
        jnp.bfloat16
    )
    total_rows = qkv.shape[1]
    queries = qkv[0, :, 0].reshape(total_rows, heads_here, HD)
    kv_block = qkv[:, :, 1:]
    visible_row = visible[0]
    score_scale = HD ** (-0.5)

    def absorb(state, incoming, offset):
        row_peak, denominator, running = state
        blocks = incoming.shape[0]
        allowed = (lax.dynamic_slice_in_dim(visible_row, offset, blocks) > 0) & (offset >= 0)
        key_rows = incoming[:, :, 0].reshape(blocks, total_rows, heads_here, HD)
        values = incoming[:, :, 1].reshape(blocks, total_rows, heads_here, HD)
        scores = (
            jnp.einsum("qhd,nkhd->qhnk", queries, key_rows, preferred_element_type=jnp.float32)
            * score_scale
        )
        allowed = allowed[None, None, :, None]
        scores = jnp.where(allowed, scores, -1e30)
        new_peak = jnp.maximum(row_peak, jnp.max(scores, axis=(2, 3)))
        probs = jnp.where(allowed, jnp.exp(scores - new_peak[:, :, None, None]), 0.0)
        rescale = jnp.exp(row_peak - new_peak)
        denominator = denominator * rescale + jnp.sum(probs, axis=(2, 3))
        weighted = jnp.einsum(
            "qhnk,nkhd->qhd", probs.astype(jnp.bfloat16), values, preferred_element_type=jnp.float32
        )
        running = running * rescale[:, :, None] + weighted
        return (new_peak, denominator, running)

    initial = (
        jnp.full((total_rows, heads_here), -1e30, jnp.float32),
        jnp.zeros((total_rows, heads_here), jnp.float32),
        jnp.zeros((total_rows, heads_here, HD), jnp.float32),
    )
    own_index = lax.axis_index("tract")
    state = absorb(initial, kv_block, own_index)
    for distance in range(1, lax.axis_size("tract")):
        moved = from_behind(kv_block, "tract", distance)
        state = absorb(state, moved, own_index - distance)
    row_peak, denominator, running = state
    attended = (
        (running / denominator[:, :, None]).astype(jnp.bfloat16).reshape(total_rows, col_width)
    )
    summed = lax.psum_scatter(
        jnp.dot(attended, w_out, preferred_element_type=jnp.float32).astype(jnp.bfloat16),
        "head",
        scatter_dimension=0,
        tiled=True,
    ).astype(jnp.float32)
    mixed = (summed * styles[2]).astype(jnp.bfloat16)
    return mixed[None]


def solution(mesh):
    placed = (
        P(("rep", "tract"), "head", None),
        P(("rep", "tract")),
        P(("rep", "tract"), None),
        P(None, None, "head"),
        P("head", None),
        P(),
    )

    def run(frames, levels, visible, w_qkv, w_out, modulation):
        n_head, n_tract, n_rep = mesh.shape["head"], mesh.shape["tract"], mesh.shape["rep"]
        tokens_here = frames.shape[1] // n_head
        weight_rows_here = w_out.shape[0] // n_head
        plane = n_tract * n_rep
        fits = (n_head, n_tract, n_rep) == (4, 4, 2) and frames.shape[2] % (2 * plane * 128) == 0
        gather = fits and weight_rows_here < tokens_here * plane
        return jax.shard_map(
            gather_body if gather else scatter_body,
            mesh=mesh,
            in_specs=placed,
            out_specs=P(("rep", "tract"), "head", None),
            check_vma=False,
        )(frames, levels, visible, w_qkv, w_out, modulation)

    return run
```

```python
import functools

import jax
import jax.numpy as jnp
from jax import lax
from jax.experimental import pallas as pl
from jax.experimental.pallas import tpu as pltpu
from jax.sharding import PartitionSpec as P

HD = 128
PLANE = ("rep", "tract")


def from_behind(value, axis, by):
    count = lax.axis_size(axis)
    pairs = [(i, i + by) for i in range(count) if 0 <= i + by < count]
    return lax.ppermute(value, axis, pairs)


def pick_styles(levels, modulation):
    n_levels = modulation.shape[0]
    chosen = (lax.iota(jnp.int32, n_levels) == levels[0]).astype(jnp.float32)
    return jnp.tensordot(chosen, modulation, axes=1, precision=lax.Precision.HIGHEST)


def attention_kernel(heads_here, q_ref, *refs):
    kv_refs, seen_ref, out_ref = refs[:-2], refs[-2], refs[-1]
    cols = heads_here * HD
    score_scale = HD ** (-0.5)
    for h in range(heads_here):
        q = q_ref[:, h * HD : (h + 1) * HD]
        scores = []
        for d, kv in enumerate(kv_refs):
            raw = lax.dot_general(
                q,
                kv[:, h * HD : (h + 1) * HD],
                (((1,), (1,)), ((), ())),
                preferred_element_type=jnp.float32,
            )
            scores.append(jnp.where(seen_ref[d] > 0, raw * score_scale, -1e30))
        peak = jnp.max(scores[0], axis=1, keepdims=True)
        for part in scores[1:]:
            peak = jnp.maximum(peak, jnp.max(part, axis=1, keepdims=True))
        denominator = jnp.zeros_like(peak)
        total = jnp.zeros((q.shape[0], HD), jnp.float32)
        for part, kv in zip(scores, kv_refs):
            probs = jnp.exp(part - peak)
            denominator += jnp.sum(probs, axis=1, keepdims=True)
            total += jnp.dot(
                probs.astype(jnp.bfloat16),
                kv[:, cols + h * HD : cols + (h + 1) * HD],
                preferred_element_type=jnp.float32,
            )
        out_ref[:, h * HD : (h + 1) * HD] = (total / denominator).astype(jnp.bfloat16)


def attend(queries, kv, seen):
    rows, cols = queries.shape
    vmem = pl.BlockSpec(memory_space=pltpu.VMEM)
    return pl.pallas_call(
        functools.partial(attention_kernel, cols // HD),
        out_shape=jax.ShapeDtypeStruct((rows, cols), jnp.bfloat16),
        in_specs=[vmem] * (1 + len(kv)) + [pl.BlockSpec(memory_space=pltpu.SMEM)],
        out_specs=vmem,
        compiler_params=pltpu.CompilerParams(vmem_limit_bytes=32 << 20),
        cost_estimate=pl.CostEstimate(
            flops=2 * rows * rows * len(kv) * cols,
            bytes_accessed=2 * rows * cols * (2 + len(kv)),
            transcendentals=rows * rows * len(kv) * cols // (2 * HD),
        ),
        name="attend",
    )(queries, *kv, seen)


def shape_kernel(level_ref, frames_ref, style_ref, out_ref, gate_ref):
    count, _, span = out_ref.shape
    floats = frames_ref[...].astype(jnp.float32)
    scale = lax.rsqrt(jnp.mean(floats * floats, axis=-1, keepdims=True) + 1e-06)
    for c in range(count):
        part = slice(c * span, (c + 1) * span)
        normed = frames_ref[:, part].astype(jnp.float32) * scale
        shaped = normed * (1.0 + style_ref[0, 1:2, part]) + style_ref[0, 0:1, part]
        out_ref[c] = shaped.astype(jnp.bfloat16)
    gate_ref[...] = style_ref[0, 2:3]


def shape_tokens(levels, frames, modulation, count):
    rows, width = frames.shape
    span = width // count
    blocks, gate = pl.pallas_call(
        shape_kernel,
        grid_spec=pltpu.PrefetchScalarGridSpec(
            num_scalar_prefetch=1,
            grid=(1,),
            in_specs=[
                pl.BlockSpec((rows, width), lambda i, level: (0, 0)),
                pl.BlockSpec((1,) + modulation.shape[1:], lambda i, level: (level[0], 0, 0)),
            ],
            out_specs=[
                pl.BlockSpec((count, rows, span), lambda i, level: (0, 0, 0)),
                pl.BlockSpec((1, width), lambda i, level: (0, 0)),
            ],
        ),
        out_shape=[
            jax.ShapeDtypeStruct((count, rows, span), jnp.bfloat16),
            jax.ShapeDtypeStruct((1, width), jnp.float32),
        ],
        compiler_params=pltpu.CompilerParams(vmem_limit_bytes=32 << 20),
        cost_estimate=pl.CostEstimate(
            flops=6 * rows * width, bytes_accessed=4 * rows * width, transcendentals=rows
        ),
        name="shape_tokens",
    )(levels, frames, modulation)
    return blocks.reshape(count * rows, span), gate


def qkv_kernel(groups, outer_ref, *refs):
    count = sum(groups)
    tokens, w_ref, out_ref, rows_ref = refs[:count], *refs[count:]
    cols = w_ref.shape[2]
    chunk = rows_ref.shape[1]
    rows = rows_ref.shape[0] // len(groups)
    total = [jnp.zeros((rows_ref.shape[0], cols), jnp.float32) for _ in range(3)]
    for k in range(w_ref.shape[1] // chunk):
        at = 0
        source = slice(k * rows, (k + 1) * rows)
        for i, size in enumerate(groups):
            block = tokens[at][source]
            if size == 2:
                block = jnp.where(outer_ref[0] > 0, block, tokens[at + 1][source])
            rows_ref[i * rows : (i + 1) * rows] = block
            at += size
        for j in range(3):
            total[j] += jnp.dot(
                rows_ref[...],
                w_ref[j, k * chunk : (k + 1) * chunk],
                preferred_element_type=jnp.float32,
            )
    for j in range(3):
        out_ref[:, j * cols : (j + 1) * cols] = total[j].astype(out_ref.dtype)


def project_qkv(outer, groups, weights, rows):
    tokens = [block for group in groups for block in group]
    chunk = tokens[0].shape[1]
    width, cols = weights.shape[1], weights.shape[2]
    total = rows * len(groups)
    vmem = pl.BlockSpec(memory_space=pltpu.VMEM)
    return pl.pallas_call(
        functools.partial(qkv_kernel, [len(group) for group in groups]),
        out_shape=jax.ShapeDtypeStruct((total, 3 * cols), jnp.bfloat16),
        in_specs=[pl.BlockSpec(memory_space=pltpu.SMEM)] + [vmem] * (len(tokens) + 1),
        out_specs=vmem,
        scratch_shapes=[pltpu.VMEM((total, chunk), jnp.bfloat16)],
        compiler_params=pltpu.CompilerParams(vmem_limit_bytes=40 << 20),
        cost_estimate=pl.CostEstimate(
            flops=6 * total * width * cols,
            bytes_accessed=6 * width * cols + 2 * total * width,
            transcendentals=0,
        ),
        name="project_qkv",
    )(outer, *tokens, weights)


def output_kernel(place_ref, att_ref, gate_ref, own_ref, *refs):
    pieces, outs, held_ref, sems = refs[:-4], refs[-4:-2], refs[-2], refs[-1]
    count = len(pieces) // 3
    span = outs[0].shape[1] // count
    width = own_ref.shape[0]
    rows = outs[0].shape[0]
    core, chip = place_ref[0] % 2, place_ref[0] // 2

    def chunk_of(delta):
        return pl.multiple_of((core * count + (chip ^ delta)) * span, 128)

    copies = []
    for delta in range(count):
        sources = [own_ref.at[:, pl.ds(chunk_of(delta), span)]]
        sources += [pieces[count * s + delta] for s in range(3)]
        copies.append(
            [
                pltpu.make_async_copy(source, held_ref.at[4 * delta + s], sems.at[4 * delta + s])
                for s, source in enumerate(sources)
            ]
        )
    for group in copies:
        for copy in group:
            copy.start()
    for delta in range(count):
        there = pl.ds(chunk_of(delta), span)
        total = jnp.zeros((2 * rows, span), jnp.float32)
        for s, copy in enumerate(copies[delta]):
            copy.wait()
            total += jnp.dot(
                att_ref[:, s * width : (s + 1) * width],
                held_ref[4 * delta + s],
                preferred_element_type=jnp.float32,
            )
        target = pl.ds(pl.multiple_of((chip ^ delta) * span, 128), span)
        for half in range(2):
            part = total[half * rows : (half + 1) * rows] * gate_ref[half : half + 1, there]
            outs[half][:, target] = part.astype(jnp.bfloat16)


def project_out(place, att, gate, own, pieces):
    rows, width = att.shape[0], own.shape[1] // 2
    count = len(pieces) // 3
    vmem = pl.BlockSpec(memory_space=pltpu.VMEM)
    anywhere = pl.BlockSpec(memory_space=pl.ANY)
    return pl.pallas_call(
        output_kernel,
        out_shape=[jax.ShapeDtypeStruct((rows // 2, width), jnp.bfloat16)] * 2,
        in_specs=[pl.BlockSpec(memory_space=pltpu.SMEM), vmem, vmem] + [anywhere] * (1 + len(pieces)),
        out_specs=[vmem, vmem],
        scratch_shapes=[
            pltpu.VMEM((4 * count,) + pieces[0].shape, jnp.bfloat16),
            pltpu.SemaphoreType.DMA((4 * count,)),
        ],
        compiler_params=pltpu.CompilerParams(vmem_limit_bytes=56 << 20),
        cost_estimate=pl.CostEstimate(
            flops=16 * rows * att.shape[1] * width,
            bytes_accessed=2 * rows * width,
            transcendentals=0,
        ),
        name="project_out",
    )(place, att, gate, own, *pieces)


def after(value, *earlier):
    return lax.optimization_barrier((value, *earlier))[0]


def gather_body(frames, levels, visible, w_qkv, w_out, modulation):
    here = lax.axis_index("head")
    n_tract = lax.axis_size("tract")
    tract = lax.axis_index("tract")
    plane = lax.axis_size("rep") * n_tract
    place = lax.axis_index("rep") * n_tract + tract
    core = lax.rem(place, 2)
    rows, width = frames.shape[1], frames.shape[2]
    cols = w_qkv.shape[2]
    span = width // plane
    outer = (here == 0) | (here == 3)
    outer_flag = outer.astype(jnp.int32)[None]
    w3 = jnp.moveaxis(w_qkv, 1, 0)

    def pair(value):
        return lax.ppermute(value, "head", [(0, 1), (1, 0), (2, 3), (3, 2)])

    def middle(value):
        return lax.ppermute(value, "head", [(1, 2), (2, 1)])

    def outward(value):
        return lax.ppermute(value, "head", [(1, 0), (2, 3)])

    def swap(value):
        return lax.ppermute(value, PLANE, [(i, i ^ 1) for i in range(plane)])

    def across_plane(piece):
        return [piece] + [
            lax.ppermute(piece, PLANE, [(i, i ^ delta) for i in range(plane)])
            for delta in range(2, plane, 2)
        ]

    chunk = core * (plane // 2) + place // 2
    piece = lax.dynamic_slice_in_dim(w_out, chunk * span, span, 1)
    w_first = pair(piece)
    w_mid = middle(piece)
    own, gate = shape_tokens(levels, frames[0], modulation, plane)
    gates = jnp.concatenate([gate, swap(gate)], axis=0)
    high = own.shape[0]

    first = pair(after(jnp.concatenate([own, w_mid], axis=0), gates))
    mid = middle(jnp.concatenate([own, w_first], axis=0))
    w_first_pieces = across_plane(w_first)
    far_mid = middle(after(first[:high], *w_first_pieces))
    out = outward(mid)
    w_second_pieces = across_plane(jnp.where(outer, first[high:], w_mid))
    far_out = outward(after(far_mid, out, *w_second_pieces))
    w_third_pieces = across_plane(jnp.where(outer, out[high:], mid[high:]))
    pieces = w_first_pieces + w_second_pieces + w_third_pieces

    early = project_qkv(outer_flag, [[own], [first], [out, mid]], w3, rows)
    late = project_qkv(outer_flag, [[far_out, far_mid]], w3, rows)
    qkv = jnp.concatenate([early, late], axis=0)
    kv_own = after(qkv[:, cols:], *w_third_pieces)
    kv_chip = from_behind(kv_own, "tract", 2)
    kv_core = lax.ppermute(kv_own, "tract", [(0, 1), (2, 3)])
    kv_both = lax.ppermute(kv_chip, "tract", [(2, 3), (3, 2)])
    sources = jnp.stack(
        [
            tract,
            jnp.where(tract % 2 == 1, tract - 1, -1),
            tract - 2,
            jnp.where(tract > 1, 3 - tract, -1),
        ]
    )
    seen = jnp.sum(
        jnp.where(sources[:, None] == lax.iota(jnp.int32, n_tract)[None, :], visible, 0), axis=1
    )
    attended = attend(
        qkv[:, :cols], [kv_own, kv_core, kv_chip, kv_both], seen
    )

    blocks = [attended[i * rows : (i + 1) * rows] for i in range(4)]
    leaving = [blocks[1], jnp.where(outer, blocks[2], blocks[3]), jnp.where(outer, blocks[3], blocks[2])]
    came = [
        lax.ppermute(value, "head", [(i, i ^ (s + 1)) for i in range(4)])
        for s, value in enumerate(leaving)
    ]
    att = jnp.concatenate(
        [blocks[0], came[0], jnp.where(outer, came[1], came[2]), jnp.where(outer, came[2], came[1])],
        axis=1,
    )
    mine, theirs = project_out(place[None], jnp.concatenate([att, swap(att)], axis=0), gates, w_out, pieces)
    theirs = swap(theirs)
    mixed = jnp.where(
        core == 0,
        jnp.concatenate([mine, theirs], axis=1),
        jnp.concatenate([theirs, mine], axis=1),
    )
    return mixed[None]


def scatter_body(frames, levels, visible, w_qkv, w_out, modulation):
    col_width = w_qkv.shape[2]
    heads_here = col_width // HD
    styles = pick_styles(levels, modulation)
    floats = lax.all_gather(frames, "head", axis=1, tiled=True).astype(jnp.float32)
    normed = floats * lax.rsqrt(jnp.mean(floats * floats, axis=-1, keepdims=True) + 1e-06)
    shaped = (normed * (1.0 + styles[1]) + styles[0]).astype(jnp.bfloat16)
    qkv = jnp.einsum("crd,dke->crke", shaped, w_qkv, preferred_element_type=jnp.float32).astype(
        jnp.bfloat16
    )
    total_rows = qkv.shape[1]
    queries = qkv[0, :, 0].reshape(total_rows, heads_here, HD)
    kv_block = qkv[:, :, 1:]
    visible_row = visible[0]
    score_scale = HD ** (-0.5)

    def absorb(state, incoming, offset):
        row_peak, denominator, running = state
        blocks = incoming.shape[0]
        allowed = (lax.dynamic_slice_in_dim(visible_row, offset, blocks) > 0) & (offset >= 0)
        key_rows = incoming[:, :, 0].reshape(blocks, total_rows, heads_here, HD)
        values = incoming[:, :, 1].reshape(blocks, total_rows, heads_here, HD)
        scores = (
            jnp.einsum("qhd,nkhd->qhnk", queries, key_rows, preferred_element_type=jnp.float32)
            * score_scale
        )
        allowed = allowed[None, None, :, None]
        scores = jnp.where(allowed, scores, -1e30)
        new_peak = jnp.maximum(row_peak, jnp.max(scores, axis=(2, 3)))
        probs = jnp.where(allowed, jnp.exp(scores - new_peak[:, :, None, None]), 0.0)
        rescale = jnp.exp(row_peak - new_peak)
        denominator = denominator * rescale + jnp.sum(probs, axis=(2, 3))
        weighted = jnp.einsum(
            "qhnk,nkhd->qhd", probs.astype(jnp.bfloat16), values, preferred_element_type=jnp.float32
        )
        running = running * rescale[:, :, None] + weighted
        return (new_peak, denominator, running)

    initial = (
        jnp.full((total_rows, heads_here), -1e30, jnp.float32),
        jnp.zeros((total_rows, heads_here), jnp.float32),
        jnp.zeros((total_rows, heads_here, HD), jnp.float32),
    )
    own_index = lax.axis_index("tract")
    state = absorb(initial, kv_block, own_index)
    for distance in range(1, lax.axis_size("tract")):
        moved = from_behind(kv_block, "tract", distance)
        state = absorb(state, moved, own_index - distance)
    row_peak, denominator, running = state
    attended = (
        (running / denominator[:, :, None]).astype(jnp.bfloat16).reshape(total_rows, col_width)
    )
    summed = lax.psum_scatter(
        jnp.dot(attended, w_out, preferred_element_type=jnp.float32).astype(jnp.bfloat16),
        "head",
        scatter_dimension=0,
        tiled=True,
    ).astype(jnp.float32)
    mixed = (summed * styles[2]).astype(jnp.bfloat16)
    return mixed[None]


def solution(mesh):
    placed = (
        P(("rep", "tract"), "head", None),
        P(("rep", "tract")),
        P(("rep", "tract"), None),
        P(None, None, "head"),
        P("head", None),
        P(),
    )

    def run(frames, levels, visible, w_qkv, w_out, modulation):
        n_head, n_tract, n_rep = mesh.shape["head"], mesh.shape["tract"], mesh.shape["rep"]
        tokens_here = frames.shape[1] // n_head
        weight_rows_here = w_out.shape[0] // n_head
        plane = n_tract * n_rep
        fits = (n_head, n_tract, n_rep) == (4, 4, 2) and frames.shape[2] % (2 * plane * 128) == 0
        gather = fits and weight_rows_here < tokens_here * plane
        return jax.shard_map(
            gather_body if gather else scatter_body,
            mesh=mesh,
            in_specs=placed,
            out_specs=P(("rep", "tract"), "head", None),
            check_vma=False,
        )(frames, levels, visible, w_qkv, w_out, modulation)

    return run
```

```python
import functools

import jax
import jax.numpy as jnp
from jax import lax
from jax.experimental import pallas as pl
from jax.experimental.pallas import tpu as pltpu
from jax.sharding import PartitionSpec as P

HD = 128
PLANE = ("rep", "tract")


def from_behind(value, axis, by):
    count = lax.axis_size(axis)
    pairs = [(i, i + by) for i in range(count) if 0 <= i + by < count]
    return lax.ppermute(value, axis, pairs)


def pick_styles(levels, modulation):
    n_levels = modulation.shape[0]
    chosen = (lax.iota(jnp.int32, n_levels) == levels[0]).astype(jnp.float32)
    return jnp.tensordot(chosen, modulation, axes=1, precision=lax.Precision.HIGHEST)


def attention_kernel(heads_here, q_ref, *refs):
    kv_refs, seen_ref, out_ref = refs[:-2], refs[-2], refs[-1]
    cols = heads_here * HD
    score_scale = HD ** (-0.5)
    for h in range(heads_here):
        q = q_ref[:, h * HD : (h + 1) * HD]
        scores = []
        for d, kv in enumerate(kv_refs):
            raw = lax.dot_general(
                q,
                kv[:, h * HD : (h + 1) * HD],
                (((1,), (1,)), ((), ())),
                preferred_element_type=jnp.float32,
            )
            scores.append(jnp.where(seen_ref[d] > 0, raw * score_scale, -1e30))
        peak = jnp.max(scores[0], axis=1, keepdims=True)
        for part in scores[1:]:
            peak = jnp.maximum(peak, jnp.max(part, axis=1, keepdims=True))
        denominator = jnp.zeros_like(peak)
        total = jnp.zeros((q.shape[0], HD), jnp.float32)
        for part, kv in zip(scores, kv_refs):
            probs = jnp.exp(part - peak)
            denominator += jnp.sum(probs, axis=1, keepdims=True)
            total += jnp.dot(
                probs.astype(jnp.bfloat16),
                kv[:, cols + h * HD : cols + (h + 1) * HD],
                preferred_element_type=jnp.float32,
            )
        out_ref[:, h * HD : (h + 1) * HD] = (total / denominator).astype(jnp.bfloat16)


def attend(queries, kv, seen):
    rows, cols = queries.shape
    vmem = pl.BlockSpec(memory_space=pltpu.VMEM)
    return pl.pallas_call(
        functools.partial(attention_kernel, cols // HD),
        out_shape=jax.ShapeDtypeStruct((rows, cols), jnp.bfloat16),
        in_specs=[vmem] * (1 + len(kv)) + [pl.BlockSpec(memory_space=pltpu.SMEM)],
        out_specs=vmem,
        compiler_params=pltpu.CompilerParams(vmem_limit_bytes=32 << 20),
        cost_estimate=pl.CostEstimate(
            flops=2 * rows * rows * len(kv) * cols,
            bytes_accessed=2 * rows * cols * (2 + len(kv)),
            transcendentals=rows * rows * len(kv) * cols // (2 * HD),
        ),
        name="attend",
    )(queries, *kv, seen)


def shape_kernel(level_ref, frames_ref, style_ref, out_ref, gate_ref):
    count, _, span = out_ref.shape
    floats = frames_ref[...].astype(jnp.float32)
    scale = lax.rsqrt(jnp.mean(floats * floats, axis=-1, keepdims=True) + 1e-06)
    for c in range(count):
        part = slice(c * span, (c + 1) * span)
        normed = frames_ref[:, part].astype(jnp.float32) * scale
        shaped = normed * (1.0 + style_ref[0, 1:2, part]) + style_ref[0, 0:1, part]
        out_ref[c] = shaped.astype(jnp.bfloat16)
    gate_ref[...] = style_ref[0, 2:3]


def shape_tokens(levels, frames, modulation, count):
    rows, width = frames.shape
    span = width // count
    blocks, gate = pl.pallas_call(
        shape_kernel,
        grid_spec=pltpu.PrefetchScalarGridSpec(
            num_scalar_prefetch=1,
            grid=(1,),
            in_specs=[
                pl.BlockSpec((rows, width), lambda i, level: (0, 0)),
                pl.BlockSpec((1,) + modulation.shape[1:], lambda i, level: (level[0], 0, 0)),
            ],
            out_specs=[
                pl.BlockSpec((count, rows, span), lambda i, level: (0, 0, 0)),
                pl.BlockSpec((1, width), lambda i, level: (0, 0)),
            ],
        ),
        out_shape=[
            jax.ShapeDtypeStruct((count, rows, span), jnp.bfloat16),
            jax.ShapeDtypeStruct((1, width), jnp.float32),
        ],
        compiler_params=pltpu.CompilerParams(vmem_limit_bytes=32 << 20),
        cost_estimate=pl.CostEstimate(
            flops=6 * rows * width, bytes_accessed=4 * rows * width, transcendentals=rows
        ),
        name="shape_tokens",
    )(levels, frames, modulation)
    return blocks.reshape(count * rows, span), gate


def qkv_kernel(groups, outer_ref, *refs):
    count = sum(groups)
    tokens, w_ref, out_ref, rows_ref = refs[:count], *refs[count:]
    cols = w_ref.shape[2]
    chunk = rows_ref.shape[1]
    rows = rows_ref.shape[0] // len(groups)
    total = [jnp.zeros((rows_ref.shape[0], cols), jnp.float32) for _ in range(3)]
    for k in range(w_ref.shape[1] // chunk):
        at = 0
        source = slice(k * rows, (k + 1) * rows)
        for i, size in enumerate(groups):
            block = tokens[at][source]
            if size == 2:
                block = jnp.where(outer_ref[0] > 0, block, tokens[at + 1][source])
            rows_ref[i * rows : (i + 1) * rows] = block
            at += size
        for j in range(3):
            total[j] += jnp.dot(
                rows_ref[...],
                w_ref[j, k * chunk : (k + 1) * chunk],
                preferred_element_type=jnp.float32,
            )
    for j in range(3):
        out_ref[:, j * cols : (j + 1) * cols] = total[j].astype(out_ref.dtype)


def project_qkv(outer, groups, weights, rows):
    tokens = [block for group in groups for block in group]
    chunk = tokens[0].shape[1]
    width, cols = weights.shape[1], weights.shape[2]
    total = rows * len(groups)
    vmem = pl.BlockSpec(memory_space=pltpu.VMEM)
    return pl.pallas_call(
        functools.partial(qkv_kernel, [len(group) for group in groups]),
        out_shape=jax.ShapeDtypeStruct((total, 3 * cols), jnp.bfloat16),
        in_specs=[pl.BlockSpec(memory_space=pltpu.SMEM)] + [vmem] * (len(tokens) + 1),
        out_specs=vmem,
        scratch_shapes=[pltpu.VMEM((total, chunk), jnp.bfloat16)],
        compiler_params=pltpu.CompilerParams(vmem_limit_bytes=40 << 20),
        cost_estimate=pl.CostEstimate(
            flops=6 * total * width * cols,
            bytes_accessed=6 * width * cols + 2 * total * width,
            transcendentals=0,
        ),
        name="project_qkv",
    )(outer, *tokens, weights)


def output_kernel(place_ref, att_ref, gate_ref, own_ref, *refs):
    pieces, out_ref = refs[:-1], refs[-1]
    count = len(pieces) // 3
    span = out_ref.shape[1] // count
    width = own_ref.shape[0]
    rows = out_ref.shape[0] // 2
    core, chip = place_ref[0] % 2, place_ref[0] // 2
    for delta in range(count):
        chunk = chip ^ delta
        start = pl.multiple_of((core * count + chunk) * span, 128)
        there = pl.ds(start, span)
        total = jnp.dot(att_ref[:, :width], own_ref[:, there], preferred_element_type=jnp.float32)
        for s in range(3):
            total += jnp.dot(
                att_ref[:, (s + 1) * width : (s + 2) * width],
                pieces[count * s + delta][...],
                preferred_element_type=jnp.float32,
            )
        target = pl.ds(pl.multiple_of(chunk * span, 128), span)
        for half in range(2):
            part = total[half * rows : (half + 1) * rows] * gate_ref[half : half + 1, there]
            out_ref[half * rows : (half + 1) * rows, target] = part.astype(jnp.bfloat16)


def project_out(place, att, gate, own, pieces):
    rows, width = att.shape[0], own.shape[1] // 2
    vmem = pl.BlockSpec(memory_space=pltpu.VMEM)
    return pl.pallas_call(
        output_kernel,
        out_shape=jax.ShapeDtypeStruct((rows, width), jnp.bfloat16),
        in_specs=[pl.BlockSpec(memory_space=pltpu.SMEM)] + [vmem] * (3 + len(pieces)),
        out_specs=vmem,
        compiler_params=pltpu.CompilerParams(vmem_limit_bytes=40 << 20),
        cost_estimate=pl.CostEstimate(
            flops=16 * rows * att.shape[1] * width,
            bytes_accessed=2 * rows * width,
            transcendentals=0,
        ),
        name="project_out",
    )(place, att, gate, own, *pieces)


def after(value, *earlier):
    return lax.optimization_barrier((value, *earlier))[0]


def gather_body(frames, levels, visible, w_qkv, w_out, modulation):
    here = lax.axis_index("head")
    n_tract = lax.axis_size("tract")
    tract = lax.axis_index("tract")
    plane = lax.axis_size("rep") * n_tract
    place = lax.axis_index("rep") * n_tract + tract
    core = lax.rem(place, 2)
    rows, width = frames.shape[1], frames.shape[2]
    cols = w_qkv.shape[2]
    span = width // plane
    outer = (here == 0) | (here == 3)
    outer_flag = outer.astype(jnp.int32)[None]
    w3 = jnp.moveaxis(w_qkv, 1, 0)

    def pair(value):
        return lax.ppermute(value, "head", [(0, 1), (1, 0), (2, 3), (3, 2)])

    def middle(value):
        return lax.ppermute(value, "head", [(1, 2), (2, 1)])

    def outward(value):
        return lax.ppermute(value, "head", [(1, 0), (2, 3)])

    def swap(value):
        return lax.ppermute(value, PLANE, [(i, i ^ 1) for i in range(plane)])

    def across_plane(piece):
        return [piece] + [
            lax.ppermute(piece, PLANE, [(i, i ^ delta) for i in range(plane)])
            for delta in range(2, plane, 2)
        ]

    chunk = core * (plane // 2) + place // 2
    piece = lax.dynamic_slice_in_dim(w_out, chunk * span, span, 1)
    w_first = pair(piece)
    w_mid = middle(piece)
    own, gate = shape_tokens(levels, frames[0], modulation, plane)
    gates = jnp.concatenate([gate, swap(gate)], axis=0)
    high = own.shape[0]

    first = pair(after(jnp.concatenate([own, w_mid], axis=0), gates))
    mid = middle(jnp.concatenate([own, w_first], axis=0))
    w_first_pieces = across_plane(w_first)
    far_mid = middle(after(first[:high], *w_first_pieces))
    out = outward(mid)
    w_second_pieces = across_plane(jnp.where(outer, first[high:], w_mid))
    far_out = outward(after(far_mid, out, *w_second_pieces))
    w_third_pieces = across_plane(jnp.where(outer, out[high:], mid[high:]))
    pieces = w_first_pieces + w_second_pieces + w_third_pieces

    early = project_qkv(outer_flag, [[own], [first], [out, mid]], w3, rows)
    late = project_qkv(outer_flag, [[far_out, far_mid]], w3, rows)
    qkv = jnp.concatenate([early, late], axis=0)
    kv_own = after(qkv[:, cols:], *w_third_pieces)
    kv_chip = from_behind(kv_own, "tract", 2)
    kv_core = lax.ppermute(kv_own, "tract", [(0, 1), (2, 3)])
    kv_both = lax.ppermute(kv_chip, "tract", [(2, 3), (3, 2)])
    sources = jnp.stack(
        [
            tract,
            jnp.where(tract % 2 == 1, tract - 1, -1),
            tract - 2,
            jnp.where(tract > 1, 3 - tract, -1),
        ]
    )
    seen = jnp.sum(
        jnp.where(sources[:, None] == lax.iota(jnp.int32, n_tract)[None, :], visible, 0), axis=1
    )
    attended = attend(
        qkv[:, :cols], [kv_own, kv_core, kv_chip, kv_both], seen
    )

    blocks = [attended[i * rows : (i + 1) * rows] for i in range(4)]
    leaving = [blocks[1], jnp.where(outer, blocks[2], blocks[3]), jnp.where(outer, blocks[3], blocks[2])]
    came = [None] * 3
    for s in (2, 1, 0):
        came[s] = lax.ppermute(leaving[s], "head", [(i, i ^ (s + 1)) for i in range(4)])
    att = jnp.concatenate(
        [blocks[0], came[0], jnp.where(outer, came[1], came[2]), jnp.where(outer, came[2], came[1])],
        axis=1,
    )
    both = project_out(place[None], jnp.concatenate([att, swap(att)], axis=0), gates, w_out, pieces)
    mine, theirs = both[:rows], swap(both[rows:])
    mixed = jnp.where(
        core == 0,
        jnp.concatenate([mine, theirs], axis=1),
        jnp.concatenate([theirs, mine], axis=1),
    )
    return mixed[None]


def scatter_body(frames, levels, visible, w_qkv, w_out, modulation):
    col_width = w_qkv.shape[2]
    heads_here = col_width // HD
    styles = pick_styles(levels, modulation)
    floats = lax.all_gather(frames, "head", axis=1, tiled=True).astype(jnp.float32)
    normed = floats * lax.rsqrt(jnp.mean(floats * floats, axis=-1, keepdims=True) + 1e-06)
    shaped = (normed * (1.0 + styles[1]) + styles[0]).astype(jnp.bfloat16)
    qkv = jnp.einsum("crd,dke->crke", shaped, w_qkv, preferred_element_type=jnp.float32).astype(
        jnp.bfloat16
    )
    total_rows = qkv.shape[1]
    queries = qkv[0, :, 0].reshape(total_rows, heads_here, HD)
    kv_block = qkv[:, :, 1:]
    visible_row = visible[0]
    score_scale = HD ** (-0.5)

    def absorb(state, incoming, offset):
        row_peak, denominator, running = state
        blocks = incoming.shape[0]
        allowed = (lax.dynamic_slice_in_dim(visible_row, offset, blocks) > 0) & (offset >= 0)
        key_rows = incoming[:, :, 0].reshape(blocks, total_rows, heads_here, HD)
        values = incoming[:, :, 1].reshape(blocks, total_rows, heads_here, HD)
        scores = (
            jnp.einsum("qhd,nkhd->qhnk", queries, key_rows, preferred_element_type=jnp.float32)
            * score_scale
        )
        allowed = allowed[None, None, :, None]
        scores = jnp.where(allowed, scores, -1e30)
        new_peak = jnp.maximum(row_peak, jnp.max(scores, axis=(2, 3)))
        probs = jnp.where(allowed, jnp.exp(scores - new_peak[:, :, None, None]), 0.0)
        rescale = jnp.exp(row_peak - new_peak)
        denominator = denominator * rescale + jnp.sum(probs, axis=(2, 3))
        weighted = jnp.einsum(
            "qhnk,nkhd->qhd", probs.astype(jnp.bfloat16), values, preferred_element_type=jnp.float32
        )
        running = running * rescale[:, :, None] + weighted
        return (new_peak, denominator, running)

    initial = (
        jnp.full((total_rows, heads_here), -1e30, jnp.float32),
        jnp.zeros((total_rows, heads_here), jnp.float32),
        jnp.zeros((total_rows, heads_here, HD), jnp.float32),
    )
    own_index = lax.axis_index("tract")
    state = absorb(initial, kv_block, own_index)
    for distance in range(1, lax.axis_size("tract")):
        moved = from_behind(kv_block, "tract", distance)
        state = absorb(state, moved, own_index - distance)
    row_peak, denominator, running = state
    attended = (
        (running / denominator[:, :, None]).astype(jnp.bfloat16).reshape(total_rows, col_width)
    )
    summed = lax.psum_scatter(
        jnp.dot(attended, w_out, preferred_element_type=jnp.float32).astype(jnp.bfloat16),
        "head",
        scatter_dimension=0,
        tiled=True,
    ).astype(jnp.float32)
    mixed = (summed * styles[2]).astype(jnp.bfloat16)
    return mixed[None]


def solution(mesh):
    placed = (
        P(("rep", "tract"), "head", None),
        P(("rep", "tract")),
        P(("rep", "tract"), None),
        P(None, None, "head"),
        P("head", None),
        P(),
    )

    def run(frames, levels, visible, w_qkv, w_out, modulation):
        n_head, n_tract, n_rep = mesh.shape["head"], mesh.shape["tract"], mesh.shape["rep"]
        tokens_here = frames.shape[1] // n_head
        weight_rows_here = w_out.shape[0] // n_head
        plane = n_tract * n_rep
        fits = (n_head, n_tract, n_rep) == (4, 4, 2) and frames.shape[2] % (2 * plane * 128) == 0
        gather = fits and weight_rows_here < tokens_here * plane
        return jax.shard_map(
            gather_body if gather else scatter_body,
            mesh=mesh,
            in_specs=placed,
            out_specs=P(("rep", "tract"), "head", None),
            check_vma=False,
        )(frames, levels, visible, w_qkv, w_out, modulation)

    return run
```
